32 devices in a mesh: pass: 4 (over z), rows: 8 (over y, x, core).
Axes of the slice: x: 2, y: 2, z: 4, core: 2. Of those that a mesh axis runs over, the one named last changes fastest.
Arguments:
- inputs: bfloat16 [4, 16, 256, 768], P('pass', 'rows'), may hold values from -6 to 6
- segment_ids: int32 [16, 256], P('rows'), may hold values from 0 to 3, never falling along the last dimension, each value on 1 to 128 neighbouring positions
- pass_embed: bfloat16 [4, 768], P('pass'), may hold values from -3 to 3
- ln1_gain: bfloat16 [768], replicated, may hold values from 0.099609375 to 1.8984375
- ln1_bias: bfloat16 [768], replicated, may hold values from -1.75 to 1.75
- w_qkv: bfloat16 [768, 2304], replicated, may hold values from -0.21875 to 0.21875
- b_query: bfloat16 [768], replicated, may hold values from -3 to 3
- b_value: bfloat16 [768], replicated, may hold values from -3 to 3
- w_out: bfloat16 [768, 768], replicated, may hold values from -0.875 to 0.875
- b_out: bfloat16 [768], replicated, may hold values from -1.75 to 1.75
- ln2_gain: bfloat16 [768], replicated, may hold values from 0.099609375 to 1.8984375
- ln2_bias: bfloat16 [768], replicated, may hold values from -1.75 to 1.75
- w_up: bfloat16 [768, 3072], replicated, may hold values from -0.21875 to 0.21875
- b_up: bfloat16 [3072], replicated, may hold values from -3 to 3
- w_down: bfloat16 [3072, 768], replicated, may hold values from -0.109375 to 0.109375
- b_down: bfloat16 [768], replicated, may hold values from -1.75 to 1.75
- cotangent: bfloat16 [4, 16, 256, 768], P('pass', 'rows'), may hold values from -6 to 6
Outputs:
- outputs: bfloat16 [4, 16, 256, 768], P('pass', 'rows')
- input_grad: bfloat16 [4, 16, 256, 768], P('pass', 'rows')
- pass_embed_grad: float32 [4, 768], P('pass', 'rows')
- ln1_gain_grad: float32 [768], P('rows')
- ln1_bias_grad: float32 [768], P('rows')
- w_qkv_grad: float32 [768, 2304], P('rows')
- b_query_grad: float32 [768], P('rows')
- b_value_grad: float32 [768], P('rows')
- w_out_grad: float32 [768, 768], P('rows')
- b_out_grad: float32 [768], P('rows')
- ln2_gain_grad: float32 [768], P('rows')
- ln2_bias_grad: float32 [768], P('rows')
- w_up_grad: float32 [768, 3072], P('rows')
- b_up_grad: float32 [3072], P('rows')
- w_down_grad: float32 [3072, 768], P('rows')
- b_down_grad: float32 [768], P('rows')
The draws below stay inside these ranges and needn't reach their ends.
Inputs may be any that keep to these rules, and one draw needn't show every extreme that they name: `segment_ids`: within each sequence the segment ids never fall; each document spans 1 to 128 positions, and one spans exactly 128.
All inputs are finite; a program needn't handle non-finite values.
Results may differ from the reference program's by a relative error of at most 0.015.
Values may be sent and summed in bfloat16 or wider, within the bound.
No kernel may reach another device: no remote copies, remote signals or barrier semaphores. Data moves between devices by JAX's collectives and lax.ppermute only.
A program may use at most 256 MiB of HBM per device.

```python
import math
import jax
import jax.numpy as jnp
import numpy as np
from jax import lax

D = 768
HEADS = 12
FF = 3072
POS = 256
NPASS = 4
SEQS = 16


def block_scale(own_key, dims, split, least, top_value):
    level = 1.0
    for position, parts in split:
        draws = jax.random.uniform(jax.random.fold_in(jax.random.fold_in(own_key, 6), position), (parts,), jnp.float32, least / len(split), top_value / len(split))
        level = level * jnp.repeat(jnp.exp(draws), dims[position] // parts).reshape((-1,) + (1,) * (len(dims) - 1 - position))
    return level


def profile(amount, total, reach, lean):
    loads = [(1 << 20) // math.isqrt(grade ** lean) + 1 for grade in range(2, amount + 1)]
    spare, counts = total - reach - (amount - 1), [1] * (amount - 1)
    while spare > 0:
        movable = [i for i in range(amount - 1) if counts[i] < reach]
        whole, remaining = sum([loads[i] for i in movable]), spare
        for i in movable:
            more = min(reach - counts[i], max(1, remaining * loads[i] // whole), spare)
            counts[i] = counts[i] + more
            spare = spare - more
    return np.array([reach] + counts)


def uneven_parts(own_key, amount, total, limit, lean):
    if amount == 2:
        one = jax.random.randint(own_key, (), max(1, total - limit), min(limit, total - 1) + 1)
        return jnp.stack([one, total - one])
    tallies = jnp.asarray(profile(amount, total, limit, lean), jnp.int32)
    pairs = (amount - 1) // 2
    donor, taker = tallies[1:1 + 2 * pairs:2], tallies[2:2 + 2 * pairs:2]
    slack = jnp.minimum(donor - 1, limit - taker)
    passed = jax.random.randint(jax.random.fold_in(own_key, 1), (pairs,), 0, 1 << 20) % (slack + 1)
    tallies = tallies.at[1:1 + 2 * pairs:2].set(donor - passed).at[2:2 + 2 * pairs:2].set(taker + passed)
    return tallies[jax.random.permutation(jax.random.fold_in(own_key, 2), amount)]


def normal_values(rng, dims, deviation, most, cuts=(), held_as=jnp.bfloat16):
    level = block_scale(rng, dims, cuts, -0.22, 0.18) if cuts else 1.0
    values = jax.random.normal(rng, dims, jnp.float32) * deviation * level
    return jnp.minimum(jnp.maximum(values, -most), most).astype(held_as)


def setup_inputs(seed: int = 0) -> dict:
    arg_keys = jax.random.split(jax.random.key(seed), 18)
    return {
        "inputs": normal_values(arg_keys[0], (NPASS, SEQS, POS, D), 1.0, 6.0, ((0, 4), (1, 8))),
        "segment_ids": jax.vmap(lambda own: jnp.searchsorted(jnp.cumsum(uneven_parts(own, 4, POS, POS // 2, 1)), jnp.arange(POS), side="right"))(jax.random.split(arg_keys[1], SEQS)).reshape((SEQS, POS)).astype(jnp.int32),
        "pass_embed": normal_values(arg_keys[2], (NPASS, D), 0.5, 3.0, ((0, 4),)),
        "ln1_gain": jnp.clip(1.0 + 0.18 * jax.random.normal(arg_keys[3], (D,), jnp.float32), 0.099609375, 1.8984375).astype(jnp.bfloat16),
        "ln1_bias": normal_values(arg_keys[4], (D,), 0.3, 1.75),
        "w_qkv": normal_values(arg_keys[5], (D, 3 * D), D ** -0.5, 0.21875),
        "b_query": normal_values(arg_keys[6], (D,), 0.5, 3.0),
        "b_value": normal_values(arg_keys[7], (D,), 0.5, 3.0),
        "w_out": normal_values(arg_keys[8], (D, D), (D // 16) ** -0.5, 0.875),
        "b_out": normal_values(arg_keys[9], (D,), 0.3, 1.75),
        "ln2_gain": jnp.clip(1.0 + 0.18 * jax.random.normal(arg_keys[10], (D,), jnp.float32), 0.099609375, 1.8984375).astype(jnp.bfloat16),
        "ln2_bias": normal_values(arg_keys[11], (D,), 0.3, 1.75),
        "w_up": normal_values(arg_keys[12], (D, FF), D ** -0.5, 0.21875),
        "b_up": normal_values(arg_keys[13], (FF,), 0.5, 3.0),
        "w_down": normal_values(arg_keys[14], (FF, D), FF ** -0.5, 0.109375),
        "b_down": normal_values(arg_keys[15], (D,), 0.3, 1.75),
        "cotangent": normal_values(arg_keys[16], (NPASS, SEQS, POS, D), 1.0, 6.0, ((0, 4), (1, 8))),
    }


@jax.custom_vjp
def low(v):
    return lax.optimization_barrier(v.astype(jnp.bfloat16)).astype(jnp.float32)

@jax.custom_vjp
def low_back(v):
    return v

def low_keep(v):
    return (low(v), None)

def low_pass(kept, grad):
    return (grad,)

def back_keep(v):
    return (v, None)

def back_low(kept, grad):
    return (low(grad),)
low.defvjp(low_keep, low_pass)
low_back.defvjp(back_keep, back_low)
EPSILON = 1e-05
MASKED = -1e+30
HIGHEST = lax.Precision.HIGHEST

def layer_norm(values, gain_vec, offset):
    average = lax.optimization_barrier(jnp.mean(values, axis=-1, keepdims=True))
    centred = values - average
    spread = lax.optimization_barrier(jnp.mean(centred * centred, axis=-1, keepdims=True))
    return centred * lax.rsqrt(spread + EPSILON) * gain_vec + offset

def attend_sequence(query_rows, key_rows, value_rows, seg_row):
    pass_count, positions, width = query_rows.shape
    head_dim = width // HEADS
    shaped = (pass_count, positions, HEADS, head_dim)
    raw = jnp.einsum('aphd,bqhd->hapbq', query_rows.reshape(shaped), key_rows.reshape(shaped), precision=HIGHEST)
    scored = low_back(raw * (1.0 / math.sqrt(head_dim)))
    places = jnp.arange(positions)
    same_doc = seg_row[:, None] == seg_row[None, :]
    earlier = places[None, :] < places[:, None]
    same_place = places[None, :] == places[:, None]
    passes = jnp.arange(pass_count)
    pass_ok = passes[None, :] <= passes[:, None]
    visible_mask = same_doc[None, :, None, :] & (earlier[None, :, None, :] | same_place[None, :, None, :] & pass_ok[:, None, :, None])
    scored = jnp.where(visible_mask[None], scored, MASKED)
    flat = scored.reshape(HEADS, pass_count * positions, pass_count * positions)
    weights = low(jax.nn.softmax(flat, axis=-1)).reshape(HEADS, pass_count, positions, pass_count, positions)
    mixed = jnp.einsum('hapbq,bqhd->aphd', weights, value_rows.reshape(shaped), precision=HIGHEST)
    return mixed.reshape(pass_count, positions, width)

def attend_piece(pieces):
    return jax.checkpoint(attend_sequence)(*pieces)

def forward(inputs_wide, params, seg_rows):
    pass_embed, ln1_gain, ln1_bias, w_qkv, b_query, b_value, w_out, b_out, ln2_gain, ln2_bias, w_up, b_up, w_down, b_down = params
    width = inputs_wide.shape[-1]
    hidden = inputs_wide + pass_embed[:, None, None, :]
    normed = low(layer_norm(hidden, ln1_gain, ln1_bias))
    joined = jnp.einsum('agpd,de->agpe', normed, w_qkv, precision=HIGHEST)
    query_rows = low_back(low(joined[..., :width] + b_query))
    key_rows = low_back(low(joined[..., width:2 * width]))
    value_rows = low_back(low(joined[..., 2 * width:] + b_value))
    mixed = lax.map(attend_piece, (jnp.swapaxes(query_rows, 0, 1), jnp.swapaxes(key_rows, 0, 1), jnp.swapaxes(value_rows, 0, 1), seg_rows))
    attended = low_back(low(jnp.swapaxes(mixed, 0, 1)))
    middle = hidden + low_back(jnp.einsum('agpd,de->agpe', attended, w_out, precision=HIGHEST) + b_out)
    normed2 = low(layer_norm(middle, ln2_gain, ln2_bias))
    inner = low_back(jnp.einsum('agpd,de->agpe', normed2, w_up, precision=HIGHEST) + b_up)
    active = low(jax.nn.gelu(inner))
    return middle + low_back(jnp.einsum('agpe,ed->agpd', active, w_down, precision=HIGHEST) + b_down)

def reference(inputs, segment_ids, pass_embed, ln1_gain, ln1_bias, w_qkv, b_query, b_value, w_out, b_out, ln2_gain, ln2_bias, w_up, b_up, w_down, b_down, cotangent):
    params = tuple((item.astype(jnp.float32) for item in (pass_embed, ln1_gain, ln1_bias, w_qkv, b_query, b_value, w_out, b_out, ln2_gain, ln2_bias, w_up, b_up, w_down, b_down)))
    group_size = 4 if SEQS % 4 == 0 else 1
    group_count = SEQS // group_size

    def regroup(array_in):
        return jnp.swapaxes(array_in.reshape(NPASS, group_count, group_size, POS, D), 0, 1)

    def ungroup(array_in):
        return jnp.swapaxes(array_in, 0, 1).reshape(NPASS, SEQS, POS, D)
    input_groups = regroup(inputs.astype(jnp.float32))
    cot_groups = regroup(cotangent.astype(jnp.float32))
    seg_groups = segment_ids.reshape(group_count, group_size, POS)
    zeros = tuple((jnp.zeros(item.shape, jnp.float32) for item in params))

    def step(totals, pieces):
        input_group, cot_group, seg_group = pieces
        result, pull = jax.vjp(lambda first, second: forward(first, second, seg_group), input_group, params)
        grad_input, grad_params = pull(cot_group)
        return (tuple((left_side + right_side for left_side, right_side in zip(totals, grad_params))), (result, grad_input))
    totals, (results, grads) = lax.scan(step, zeros, (input_groups, cot_groups, seg_groups))
    outputs = ungroup(results).astype(jnp.bfloat16)
    input_grad = ungroup(grads).astype(jnp.bfloat16)
    return (outputs, input_grad, totals[0], totals[1], totals[2], totals[3], totals[4], totals[5], totals[6], totals[7], totals[8], totals[9], totals[10], totals[11], totals[12], totals[13])
```

```python
import math

import jax
import jax.numpy as jnp
from jax import lax
from jax.experimental import pallas as pl
from jax.experimental.pallas import tpu as pltpu
from jax.sharding import PartitionSpec as P

HEADS = 12
EPSILON = 1e-05
MASKED = -1e30
BLOCK = 64
SPAN = 128
VMEM_LIMIT = 56 * 1024 * 1024
AXES = ("pass", "rows")
BF16, F32 = jnp.bfloat16, jnp.float32

LN1_GAIN, LN1_BIAS, B_OUT, LN2_GAIN, LN2_BIAS, B_DOWN, EMBED_A, EMBED_B = range(8)


def nn(left, right):
    return jnp.dot(left, right, preferred_element_type=F32)


def nt(left, right):
    return lax.dot_general(left, right, (((1,), (1,)), ((), ())), preferred_element_type=F32)


def tn(left, right):
    return lax.dot_general(left, right, (((0,), (0,)), ((), ())), preferred_element_type=F32)


def normalise(values):
    average = jnp.mean(values, axis=-1, keepdims=True)
    centred = values - average
    spread = jnp.mean(centred * centred, axis=-1, keepdims=True)
    scale = lax.rsqrt(spread + EPSILON)
    return centred * scale, scale


def params(**more):
    return pltpu.CompilerParams(vmem_limit_bytes=VMEM_LIMIT, **more)


def whole(shape):
    return pl.BlockSpec(shape, lambda *_: (0,) * len(shape))


def pieces(positions):
    for block in range(positions // BLOCK):
        for half in range(2):
            yield half, block * BLOCK, (2 * block + half) * BLOCK


def hidden_piece(xa, xb, vecs, half, start):
    source = xb if half else xa
    row = EMBED_B if half else EMBED_A
    return source[start : start + BLOCK, :].astype(F32) + vecs[row : row + 1, :]


def key_value_kernel(xa, xb, vecs, w, bias, out, normed):
    @pl.when(pl.program_id(0) == 0)
    def _():
        for half, start, at in pieces(xa.shape[0]):
            unit, _ = normalise(hidden_piece(xa, xb, vecs, half, start))
            scaled = unit * vecs[LN1_GAIN : LN1_GAIN + 1, :] + vecs[LN1_BIAS : LN1_BIAS + 1, :]
            normed[at : at + BLOCK, :] = scaled.astype(BF16)

    out[...] = (nn(normed[...], w[...]) + bias[...]).astype(BF16)


def query_kernel(normed, w, bias, out):
    out[...] = (nn(normed[...], w[...]) + bias[...]).astype(BF16)


def join_sources(own, other, target):
    for block in range(own.shape[0] // SPAN):
        target[2 * block * SPAN : (2 * block + 1) * SPAN, :] = own[block * SPAN : (block + 1) * SPAN, :]
        target[(2 * block + 1) * SPAN : (2 * block + 2) * SPAN, :] = other[block * SPAN : (block + 1) * SPAN, :]


def stack_heads(rows):
    lane = lax.broadcasted_iota(jnp.int32, rows.shape, 1)
    zero = jnp.zeros_like(rows)
    half = rows.shape[1] // 2
    return jnp.concatenate([jnp.where(lane < half, rows, zero), jnp.where(lane >= half, rows, zero)], axis=0)


def unstack_columns(pair):
    return jnp.concatenate([pair[:BLOCK, :SPAN], pair[BLOCK:, SPAN:]], axis=0)


def key_range(block):
    first = max(block - 2, 0)
    return first, 2 * SPAN * first, 2 * SPAN * (block + 1)


def attend_kernel(q, k_own, v_own, k_other, v_other, bias, out, log_total, keys, values_t, values):
    scaling = 1.0 / math.sqrt(BLOCK)
    join_sources(k_own, k_other, keys)
    join_sources(v_own, v_other, values)
    values_t[...] = values[...].T
    for block in range(q.shape[0] // SPAN):
        first, low, high = key_range(block)
        skip = 2 * SPAN * (first - (block - 2))
        stacked = stack_heads(q[block * SPAN : (block + 1) * SPAN, :] * scaling)
        shown = bias[block, skip:, :]
        scored = nt(keys[low:high, :], stacked) + jnp.concatenate([shown, shown], axis=1)
        highest = jnp.max(scored, axis=0, keepdims=True)
        exponent = jnp.exp(scored - highest)
        total = jnp.sum(exponent, axis=0, keepdims=True)
        mixed = nn(values_t[:, low:high], exponent.astype(BF16)) / total
        out[block * SPAN : (block + 1) * SPAN, :] = unstack_columns(mixed).T.astype(BF16)
        logs = highest + jnp.log(total)
        log_total[0, 2 * block : 2 * block + 1, :] = logs[:, :SPAN]
        log_total[0, 2 * block + 1 : 2 * block + 2, :] = logs[:, SPAN:]


def attend_back_kernel(
    q, k_own, v_own, k_other, v_other, bias, log_total, attended, grad,
    dq, dk_own, dv_own, dk_other, dv_other,
    keys, values, keys_t, dk, dv,
):
    scaling = 1.0 / math.sqrt(BLOCK)
    join_sources(k_own, k_other, keys)
    join_sources(v_own, v_other, values)
    keys_t[...] = keys[...].T
    dk[...] = jnp.zeros_like(dk)
    dv[...] = jnp.zeros_like(dv)
    for block in range(q.shape[0] // SPAN):
        first, low, high = key_range(block)
        skip = 2 * SPAN * (first - (block - 2))
        rows = slice(block * SPAN, (block + 1) * SPAN)
        stacked = stack_heads(q[rows, :] * scaling)
        grads = grad[rows, :]
        stacked_grads = stack_heads(grads)
        product = (grads.astype(F32) * attended[rows, :].astype(F32)).T
        centre = jnp.concatenate(
            [jnp.sum(product[:BLOCK], axis=0, keepdims=True), jnp.sum(product[BLOCK:], axis=0, keepdims=True)], axis=1
        )
        logs = jnp.concatenate(
            [log_total[0, 2 * block : 2 * block + 1, :], log_total[0, 2 * block + 1 : 2 * block + 2, :]], axis=1
        )
        shown = bias[block, skip:, :]
        scored = nt(keys[low:high, :], stacked) + jnp.concatenate([shown, shown], axis=1)
        weights = jnp.exp(scored - logs)
        grad_weights = nt(values[low:high, :], stacked_grads)
        grad_scored = (weights * (grad_weights - centre)).astype(BF16)
        dv[low:high, :] += nn(weights.astype(BF16), stacked_grads)
        dk[low:high, :] += nn(grad_scored, stacked)
        dq_pair = nn(keys_t[:, low:high], grad_scored) * scaling
        dq[rows, :] = unstack_columns(dq_pair).T.astype(BF16)
    for block in range(q.shape[0] // SPAN):
        rows = slice(block * SPAN, (block + 1) * SPAN)
        own, other = slice(2 * block * SPAN, (2 * block + 1) * SPAN), slice((2 * block + 1) * SPAN, (2 * block + 2) * SPAN)
        dk_own[rows, :] = dk[own, :].astype(BF16)
        dv_own[rows, :] = dv[own, :].astype(BF16)
        dk_other[rows, :] = dk[other, :].astype(BF16)
        dv_other[rows, :] = dv[other, :].astype(BF16)


def feed_forward_kernel(
    attended, xa, xb, ca, cb, vecs, w_out, w_up, b_up, w_down,
    out_a, out_b, grad_middle, grad_attended, w_out_grad, w_up_grad, w_down_grad, b_up_grad, small,
    middle, normed2, normed2_t, cot, acc_out, acc_grad,
):
    step = pl.program_id(0)
    positions = xa.shape[0]

    @pl.when(step == 0)
    def _():
        branch = nn(attended[...], w_out[...]) + vecs[B_OUT : B_OUT + 1, :]
        for half, start, at in pieces(positions):
            mid = hidden_piece(xa, xb, vecs, half, start) + branch[at : at + BLOCK, :]
            middle[at : at + BLOCK, :] = mid
            unit, _ = normalise(mid)
            scaled = unit * vecs[LN2_GAIN : LN2_GAIN + 1, :] + vecs[LN2_BIAS : LN2_BIAS + 1, :]
            normed2[at : at + BLOCK, :] = scaled.astype(BF16)
            cot[at : at + BLOCK, :] = (cb if half else ca)[start : start + BLOCK, :]
        normed2_t[...] = normed2[...].T
        acc_out[...] = jnp.zeros_like(acc_out)
        acc_grad[...] = jnp.zeros_like(acc_grad)

    inner = nn(normed2[...], w_up[...]) + b_up[...]
    rate = math.sqrt(2 / math.pi)
    square = inner * inner
    bent = jnp.tanh(rate * inner * (1.0 + 0.044715 * square))
    open_half = 0.5 + 0.5 * bent
    active = (inner * open_half).astype(BF16)
    slope = open_half + 0.5 * inner * (1.0 - bent * bent) * (rate + (3 * 0.044715 * rate) * square)
    grad_inner_wide = nt(cot[...], w_down[...]) * slope
    grad_inner = grad_inner_wide.astype(BF16)
    b_up_grad[...] = jnp.sum(grad_inner.astype(F32), axis=0, keepdims=True)
    acc_out[...] += nn(active, w_down[...])
    acc_grad[...] += nt(grad_inner, w_up[...])
    w_down_grad[...] = tn(active, cot[...]).astype(BF16)
    w_up_grad[...] = nn(normed2_t[...], grad_inner).astype(BF16)

    @pl.when(step == pl.num_programs(0) - 1)
    def _():
        width = middle.shape[1]
        sums = [jnp.zeros((1, width), F32) for _ in range(4)]
        for half, start, at in pieces(positions):
            rows = slice(at, at + BLOCK)
            mid = middle[rows, :]
            result = mid + acc_out[rows, :] + vecs[B_DOWN : B_DOWN + 1, :]
            (out_b if half else out_a)[start : start + BLOCK, :] = result.astype(BF16)
            unit, scale = normalise(mid)
            grad_norm = acc_grad[rows, :]
            cot_wide = cot[rows, :].astype(F32)
            scaled = grad_norm * vecs[LN2_GAIN : LN2_GAIN + 1, :]
            mean_scaled = jnp.mean(scaled, axis=-1, keepdims=True)
            mean_unit = jnp.mean(scaled * unit, axis=-1, keepdims=True)
            grad_mid = cot_wide + scale * (scaled - mean_scaled - unit * mean_unit)
            grad_middle[rows, :] = grad_mid
            branch = grad_mid.astype(BF16)
            normed2[rows, :] = branch
            for i, term in enumerate((cot_wide, grad_norm * unit, grad_norm, branch.astype(F32))):
                sums[i] = sums[i] + jnp.sum(term, axis=0, keepdims=True)
        small[...] = jnp.concatenate(sums + [jnp.zeros((4, width), F32)], axis=0)
        grad_attended[...] = nt(normed2[...], w_out[...]).astype(BF16)
        w_out_grad[...] = tn(attended[...], normed2[...]).astype(BF16)


def project_back_kernel(
    dq, dk_own, dv_own, dk_in, dv_in, normed, grad_middle, xa, xb, vecs, w,
    w_grad, out_a, out_b, small,
    normed_t, joined, acc,
):
    step = pl.program_id(0)
    width = normed.shape[1]

    @pl.when(step == 0)
    def _():
        normed_t[...] = normed[...].T
        joined[...] = dq[...]
        small[...] = jnp.zeros_like(small)
        small[0:1, :] = jnp.sum(dq[...].astype(F32), axis=0, keepdims=True)

    @pl.when(step == 1)
    def _():
        joined[...] = (dk_own[...].astype(F32) + dk_in[...].astype(F32)).astype(BF16)

    @pl.when(step == 2)
    def _():
        total = (dv_own[...].astype(F32) + dv_in[...].astype(F32)).astype(BF16)
        joined[...] = total
        small[1:2, :] = jnp.sum(total.astype(F32), axis=0, keepdims=True)

    w_grad[...] = nn(normed_t[...], joined[...]).astype(BF16)
    part = nt(joined[...], w[...])

    @pl.when(step == 0)
    def _():
        acc[...] = part

    @pl.when(step > 0)
    def _():
        acc[...] += part

    @pl.when(step == pl.num_programs(0) - 1)
    def _():
        sums = [jnp.zeros((1, width), F32) for _ in range(4)]
        for half, start, at in pieces(xa.shape[0]):
            rows = slice(at, at + BLOCK)
            unit, scale = normalise(hidden_piece(xa, xb, vecs, half, start))
            grad_norm = acc[rows, :]
            scaled = grad_norm * vecs[LN1_GAIN : LN1_GAIN + 1, :]
            mean_scaled = jnp.mean(scaled, axis=-1, keepdims=True)
            mean_unit = jnp.mean(scaled * unit, axis=-1, keepdims=True)
            grad_hidden = grad_middle[rows, :] + scale * (scaled - mean_scaled - unit * mean_unit)
            (out_b if half else out_a)[start : start + BLOCK, :] = grad_hidden.astype(BF16)
            sums[0] = sums[0] + jnp.sum(grad_norm * unit, axis=0, keepdims=True)
            sums[1] = sums[1] + jnp.sum(grad_norm, axis=0, keepdims=True)
            sums[2 + half] = sums[2 + half] + jnp.sum(grad_hidden, axis=0, keepdims=True)
        small[2:6, :] = jnp.concatenate(sums, axis=0)


def pick(array, index, axis):
    return lax.dynamic_index_in_dim(array, index, axis, keepdims=False)


def on_device(
    inputs,
    segment_ids,
    pass_embed,
    ln1_gain,
    ln1_bias,
    w_qkv,
    b_query,
    b_value,
    w_out,
    b_out,
    ln2_gain,
    ln2_bias,
    w_up,
    b_up,
    w_down,
    b_down,
    cotangent,
):
    pass_count, row_count = lax.axis_size("pass"), lax.axis_size("rows")
    place, row = lax.axis_index("pass"), lax.axis_index("rows")
    core = row % 2
    _, sequences, positions, width = inputs.shape
    hidden_units = w_up.shape[1]
    tokens = 2 * positions
    blocks = positions // BLOCK
    pairs = width // SPAN
    assert pass_count == 4 and sequences == 2 and width == HEADS * BLOCK and row_count % 2 == 0

    def numbered(r, k):
        return r * row_count + k

    def permutation(target):
        return [
            (numbered(r, k), numbered(*target(r, k))) for r in range(pass_count) for k in range(row_count)
        ]

    def inverse(pairs_of):
        return [(b, a) for a, b in pairs_of]

    def to_a(r, k):
        return 2 * (k % 2) + r % 2, k - k % 2 + r // 2

    def to_b(r, k):
        return 2 * (k % 2) + 1 - r % 2, k - k % 2 + r // 2

    go_a, go_b = permutation(to_a), permutation(to_b)
    back_a, back_b = inverse(go_a), inverse(go_b)
    other_core = permutation(lambda r, k: (r, k ^ 1))

    def move(array, perm):
        return lax.ppermute(array, AXES, perm)

    low = place % 2
    xa = move(pick(inputs[0], low, 0), go_a)
    xb = move(pick(inputs[0], 1 - low, 0), go_b)
    embed = pass_embed.astype(F32)
    seg = segment_ids.reshape(sequences, 1, positions)
    embed_a, embed_b = move(embed, go_a), move(embed, go_b)
    seg_a = move(pick(seg, low, 0), go_a)[0]
    ca = move(pick(cotangent[0], low, 0), go_a)
    cb = move(pick(cotangent[0], 1 - low, 0), go_b)

    vecs = jnp.concatenate(
        [v.astype(F32).reshape(1, width) for v in (ln1_gain, ln1_bias, b_out, ln2_gain, ln2_bias, b_down)]
        + [embed_a, embed_b],
        axis=0,
    )
    bias_qkv = jnp.concatenate([b_query.astype(F32), jnp.zeros((width,), F32), b_value.astype(F32)]).reshape(1, -1)

    def passes_of(which_core):
        return jnp.stack([2 * which_core + low, 2 * which_core + 1 - low])

    own_passes = passes_of(core)
    key_passes = jnp.stack([own_passes, passes_of(1 - core)])
    padded = jnp.concatenate([jnp.full((2 * BLOCK,), -1, jnp.int32), seg_a])
    seg_q = seg_a.reshape(blocks, BLOCK)
    seg_k = jnp.stack([padded[i * BLOCK : (i + 3) * BLOCK] for i in range(blocks)]).reshape(blocks, 3, BLOCK)
    pos_q = jnp.arange(positions).reshape(blocks, BLOCK)
    pos_k = pos_q[:, None, :] + (jnp.arange(3) * BLOCK - 2 * BLOCK)[None, :, None]

    def over_keys(a):
        return a[:, :, None, None, :, None, None]

    def over_queries(a):
        return a[:, None, None, None, None, None, :]

    pass_ok = key_passes[None, None, :, :, None, None, None] <= own_passes[None, None, None, None, None, :, None]
    shown = (over_keys(seg_k) == over_queries(seg_q)) & (
        (over_keys(pos_k) < over_queries(pos_q)) | ((over_keys(pos_k) == over_queries(pos_q)) & pass_ok)
    )
    bias = jnp.where(shown, 0.0, MASKED).astype(F32).reshape(blocks, 3 * 2 * SPAN, SPAN)

    part = width // 2
    kv, normed = pl.pallas_call(
        key_value_kernel,
        grid=(2 * width // part,),
        in_specs=[
            whole((positions, width)),
            whole((positions, width)),
            whole(vecs.shape),
            pl.BlockSpec((width, part), lambda i: (0, i + width // part)),
            pl.BlockSpec((1, part), lambda i: (0, i + width // part)),
        ],
        out_specs=[pl.BlockSpec((tokens, part), lambda i: (0, i)), whole((tokens, width))],
        out_shape=[
            jax.ShapeDtypeStruct((tokens, 2 * width), BF16),
            jax.ShapeDtypeStruct((tokens, width), BF16),
        ],
        compiler_params=params(),
        name="norm_key_value",
    )(xa, xb, vecs, w_qkv, bias_qkv)
    kv_other = move(kv, other_core)
    query = pl.pallas_call(
        query_kernel,
        grid=(width // part,),
        in_specs=[
            whole((tokens, width)),
            pl.BlockSpec((width, part), lambda i: (0, i)),
            pl.BlockSpec((1, part), lambda i: (0, i)),
        ],
        out_specs=pl.BlockSpec((tokens, part), lambda i: (0, i)),
        out_shape=jax.ShapeDtypeStruct((tokens, width), BF16),
        compiler_params=params(),
        name="query",
    )(normed, w_qkv, bias_qkv)

    def pair_spec(offset=0):
        return pl.BlockSpec((tokens, SPAN), lambda i: (0, i + offset))

    log_spec = pl.BlockSpec((1, 2 * blocks, SPAN), lambda i: (i, 0, 0))
    attended, logs = pl.pallas_call(
        attend_kernel,
        grid=(pairs,),
        in_specs=[pair_spec(), pair_spec(), pair_spec(pairs), pair_spec(), pair_spec(pairs), whole(bias.shape)],
        out_specs=[pair_spec(), log_spec],
        out_shape=[
            jax.ShapeDtypeStruct((tokens, width), BF16),
            jax.ShapeDtypeStruct((pairs, 2 * blocks, SPAN), F32),
        ],
        scratch_shapes=[
            pltpu.VMEM((2 * tokens, SPAN), BF16),
            pltpu.VMEM((SPAN, 2 * tokens), BF16),
            pltpu.VMEM((2 * tokens, SPAN), BF16),
        ],
        compiler_params=params(),
        name="attend",
    )(query, kv, kv, kv_other, kv_other, bias)

    block_up = 384
    out_a, out_b, grad_middle, grad_attended, w_out_grad, w_up_grad, w_down_grad, b_up_grad, small2 = pl.pallas_call(
        feed_forward_kernel,
        grid=(hidden_units // block_up,),
        in_specs=[
            whole((tokens, width)),
            whole((positions, width)),
            whole((positions, width)),
            whole((positions, width)),
            whole((positions, width)),
            whole(vecs.shape),
            whole((width, width)),
            pl.BlockSpec((width, block_up), lambda i: (0, i)),
            pl.BlockSpec((1, block_up), lambda i: (0, i)),
            pl.BlockSpec((block_up, width), lambda i: (i, 0)),
        ],
        out_specs=[
            whole((positions, width)),
            whole((positions, width)),
            whole((tokens, width)),
            whole((tokens, width)),
            whole((width, width)),
            pl.BlockSpec((width, block_up), lambda i: (0, i)),
            pl.BlockSpec((block_up, width), lambda i: (i, 0)),
            pl.BlockSpec((1, block_up), lambda i: (0, i)),
            whole((8, width)),
        ],
        out_shape=[
            jax.ShapeDtypeStruct((positions, width), BF16),
            jax.ShapeDtypeStruct((positions, width), BF16),
            jax.ShapeDtypeStruct((tokens, width), F32),
            jax.ShapeDtypeStruct((tokens, width), BF16),
            jax.ShapeDtypeStruct((width, width), BF16),
            jax.ShapeDtypeStruct((width, hidden_units), BF16),
            jax.ShapeDtypeStruct((hidden_units, width), BF16),
            jax.ShapeDtypeStruct((1, hidden_units), F32),
            jax.ShapeDtypeStruct((8, width), F32),
        ],
        scratch_shapes=[
            pltpu.VMEM((tokens, width), F32),
            pltpu.VMEM((tokens, width), BF16),
            pltpu.VMEM((width, tokens), BF16),
            pltpu.VMEM((tokens, width), BF16),
            pltpu.VMEM((tokens, width), F32),
            pltpu.VMEM((tokens, width), F32),
        ],
        compiler_params=params(),
        name="feed_forward",
    )(attended, xa, xb, ca, cb, vecs, w_out, w_up, b_up.astype(F32).reshape(1, -1), w_down)

    back_out_a, back_out_b = move(out_a, back_a), move(out_b, back_b)

    dq, dk_own, dv_own, dk_other, dv_other = pl.pallas_call(
        attend_back_kernel,
        grid=(pairs,),
        in_specs=[pair_spec(), pair_spec(), pair_spec(pairs), pair_spec(), pair_spec(pairs), whole(bias.shape)]
        + [log_spec, pair_spec(), pair_spec()],
        out_specs=[pair_spec()] * 5,
        out_shape=[jax.ShapeDtypeStruct((tokens, width), BF16)] * 5,
        scratch_shapes=[
            pltpu.VMEM((2 * tokens, SPAN), BF16),
            pltpu.VMEM((2 * tokens, SPAN), BF16),
            pltpu.VMEM((SPAN, 2 * tokens), BF16),
            pltpu.VMEM((2 * tokens, SPAN), F32),
            pltpu.VMEM((2 * tokens, SPAN), F32),
        ],
        compiler_params=params(),
        name="attend_back",
    )(query, kv, kv, kv_other, kv_other, bias, logs, attended, grad_attended)
    dk_in, dv_in = move(dk_other, other_core), move(dv_other, other_core)

    w_qkv_grad, in_a, in_b, small1 = pl.pallas_call(
        project_back_kernel,
        grid=(3,),
        in_specs=[whole((tokens, width))] * 7
        + [
            whole((positions, width)),
            whole((positions, width)),
            whole(vecs.shape),
            pl.BlockSpec((width, width), lambda i: (0, i)),
        ],
        out_specs=[
            pl.BlockSpec((width, width), lambda i: (0, i)),
            whole((positions, width)),
            whole((positions, width)),
            whole((8, width)),
        ],
        out_shape=[
            jax.ShapeDtypeStruct((width, 3 * width), BF16),
            jax.ShapeDtypeStruct((positions, width), BF16),
            jax.ShapeDtypeStruct((positions, width), BF16),
            jax.ShapeDtypeStruct((8, width), F32),
        ],
        scratch_shapes=[
            pltpu.VMEM((width, tokens), BF16),
            pltpu.VMEM((tokens, width), BF16),
            pltpu.VMEM((tokens, width), F32),
        ],
        compiler_params=params(),
        name="project_back",
    )(dq, dk_own, dv_own, dk_in, dv_in, normed, grad_middle, xa, xb, vecs, w_qkv)
    back_in_a, back_in_b = move(in_a, back_a), move(in_b, back_b)

    def put_back(first, second):
        both = jnp.stack([first, second])
        return jnp.where(low == 0, both, both[::-1])[None]

    outputs = put_back(back_out_a, back_out_b)
    input_grad = put_back(back_in_a, back_in_b)

    bits = [1 << i for i in range(1, row_count.bit_length() - 1)]
    flips = {bit: permutation(lambda r, k, bit=bit: (r, k ^ bit)) for bit in bits}
    near = permutation(lambda r, k: (r ^ 1, k))
    far = permutation(lambda r, k: (r ^ 2, k))

    def scatter_sum(grad):
        rows_in, columns = grad.shape
        shards = grad.reshape(row_count // 2, 2, rows_in // row_count, columns)
        held = pick(shards, core, 1) + move(pick(shards, 1 - core, 1), other_core)
        half = columns // 2
        finished = []
        for order, piece in ((bits, held[..., :half]), (bits[::-1], held[..., half:])):
            axes = bits[::-1]
            piece = piece.reshape((2,) * len(axes) + piece.shape[1:])
            for bit in order:
                at = axes.index(bit)
                mine = (row // bit) % 2
                piece = pick(piece, mine, at) + move(pick(piece, 1 - mine, at), flips[bit])
                axes = axes[:at] + axes[at + 1 :]
            finished.append(piece)
        first, second = finished
        even = low == 0
        held = jnp.where(even, first, second) + move(jnp.where(even, second, first), near)
        held = held + move(held, far)
        other = move(held, near)
        return jnp.concatenate(
            [jnp.where(even, held, other), jnp.where(even, other, held)], axis=-1
        ).astype(F32)

    w_down_sum = scatter_sum(w_down_grad)
    w_up_sum = scatter_sum(w_up_grad)
    w_out_sum = scatter_sum(w_out_grad)
    w_qkv_sum = scatter_sum(w_qkv_grad)

    which = jnp.arange(pass_count)[:, None]
    embeds = jnp.where(which == own_passes[0], small1[4:5], 0.0) + jnp.where(which == own_passes[1], small1[5:6], 0.0)
    vectors = jnp.concatenate([small2[:4], small1[:4], b_up_grad.reshape(-1, width), embeds], axis=0)
    for perm in [other_core] + [flips[bit] for bit in bits] + [near, far]:
        vectors = vectors + move(vectors, perm)

    def shard_of(vector):
        size = vector.shape[-1] // row_count
        return lax.dynamic_slice_in_dim(vector, row * size, size, axis=vector.ndim - 1)

    shards = shard_of(vectors[:8])
    ups = hidden_units // width
    b_up_sum = shard_of(vectors[8 : 8 + ups].reshape(-1))
    embed_sum = shard_of(pick(vectors[8 + ups :], place, 0).reshape(1, width))
    return (
        outputs,
        input_grad,
        embed_sum,
        shards[6],
        shards[7],
        w_qkv_sum,
        shards[4],
        shards[5],
        w_out_sum,
        shards[3],
        shards[1],
        shards[2],
        w_up_sum,
        b_up_sum,
        w_down_sum,
        shards[0],
    )


def solution(mesh):
    placed = (
        P("pass", "rows", None, None),
        P("rows", None),
        P("pass", None),
        P(),
        P(),
        P(),
        P(),
        P(),
        P(),
        P(),
        P(),
        P(),
        P(),
        P(),
        P(),
        P(),
        P("pass", "rows", None, None),
    )
    return jax.shard_map(
        on_device,
        mesh=mesh,
        in_specs=placed,
        out_specs=(
            P("pass", "rows", None, None),
            P("pass", "rows", None, None),
            P("pass", "rows"),
            P("rows"),
            P("rows"),
            P("rows", None),
            P("rows"),
            P("rows"),
            P("rows", None),
            P("rows"),
            P("rows"),
            P("rows"),
            P("rows", None),
            P("rows"),
            P("rows", None),
            P("rows"),
        ),
        check_vma=False,
    )
```
